32 devices in a mesh: parts: 2 (over x), gx: 8 (over z, y), gy: 2 (over core).
Axes of the slice: x: 2, y: 2, z: 4, core: 2. Of those that a mesh axis runs over, the one named last changes fastest.
Arguments:
- tokens: float32 [1024, 8192], P(('parts', 'gy'), 'gx'), parts along dimension 0, may hold values from -6 to 6
- gate_up_weight: bfloat16 [2, 8192, 16384], P(None, 'gx', 'gy'), may hold values from -0.0625 to 0.0625
- down_weight: bfloat16 [16384, 8192], P('gy', 'gx'), may hold values from -0.046875 to 0.046875
Outputs:
- block_out: float32 [1024, 8192], P(('parts', 'gy'), 'gx'), parts along dimension 0
The draws below stay inside these ranges and needn't reach their ends.
There are 2 independent parts, one for each index of `parts`. The reference program is written for one: setup_inputs(seed, part) draws one part's arguments, and reference() takes and returns one part's arrays. A program takes and returns all parts, laid end to end along the dimension named above; an argument that names none is the same for every part. Nothing has to cross between parts.
All inputs are finite; a program needn't handle non-finite values.
Results may differ from the reference program's by a relative error of at most 0.0051.
Values may be sent and summed in bfloat16 or wider, within the bound.
A program may use at most 256 MiB of HBM per device.

```python
import jax
import jax.numpy as jnp

D = 8192
FF_DEV = 8192
ROWS = 512
FF = 16384
N_GY = 2


def steps_of(rng, dims, cuts, least, largest):
    gain = 1.0
    for dim, blocks in cuts:
        draws = jax.random.uniform(jax.random.fold_in(jax.random.fold_in(rng, 6), dim), (blocks,), jnp.float32, least / len(cuts), largest / len(cuts))
        gain = gain * jnp.repeat(jnp.exp(draws), dims[dim] // blocks).reshape((-1,) + (1,) * (len(dims) - 1 - dim))
    return gain


def noise(rng, extent, width, limit, pieces=(), kind=jnp.bfloat16):
    drawn = jax.random.normal(rng, extent, jnp.float32) * width
    if len(pieces) > 0:
        drawn = steps_of(rng, extent, pieces, -0.22, 0.18) * drawn
    return jnp.clip(drawn, min=-limit, max=limit).astype(kind)


def setup_inputs(seed: int = 0, part: int = 0) -> dict:
    seeds = jax.random.split(jax.random.key(seed), 4)
    part_splits = jax.random.split(jax.random.fold_in(seeds[3], part), 4)
    return {
        "tokens": noise(part_splits[0], (ROWS, D), 1.0, 6.0, ((0, 2), (1, 8)), jnp.float32),
        "gate_up_weight": noise(seeds[1], (2, D, FF), D ** -0.5, 0.0625, ((1, 8), (2, 2))),
        "down_weight": noise(seeds[2], (FF, D), (FF_DEV * N_GY) ** -0.5, 0.046875, ((0, 2), (1, 8))),
    }


def reference(tokens, gate_up_weight, down_weight):
    rounded = tokens.astype(jnp.bfloat16)
    gate = jnp.dot(rounded, gate_up_weight[0], preferred_element_type=jnp.float32)
    up = jnp.dot(rounded, gate_up_weight[1], preferred_element_type=jnp.float32)
    hidden = (jax.nn.silu(gate) * up).astype(jnp.bfloat16)
    return jnp.dot(hidden, down_weight, preferred_element_type=jnp.float32)
```

```python
import functools

import jax
import jax.numpy as jnp
from jax import lax
from jax.experimental import pallas as pl
from jax.experimental.pallas import tpu as pltpu
from jax.sharding import PartitionSpec as P

WIDTH = 256
SLOTS = 4


def kernel(
    n, pair, chunks, tok_in, w_ref, d_ref, o_ref,
    tok, wbuf, dbuf, ysend, yrecv, zrecv, own, hid, acc, rbuf,
    wsem, dsem, tsem, ys, yr, zs, zr, gs, gr, fs, fr, osem,
):
    far = n // pair
    w = hid.shape[-1]
    block = chunks * w
    tiles = chunks * far
    me = lax.axis_index("gx")
    core = lax.axis_index("gy")
    z, y = me // pair, lax.rem(me, pair)
    other = 1 - y
    mate = {"gy": 1 - core}

    def place(zz, yy):
        return zz * pair + yy

    def ahead(i):
        return lax.rem(z + 1 + i, far)

    def behind(j):
        return lax.rem(z - j + far, far)

    near = {"gx": place(z, other)}

    def weights(t):
        slot = lax.rem(t, SLOTS)
        side = jnp.where(t < tiles, other, y)
        r = lax.rem(t, tiles)
        dest = place(ahead(lax.rem(r, far)), side)
        col = pl.multiple_of(dest * block + (r // far) * w, 128)
        return [
            pltpu.make_async_copy(
                w_ref.at[k, :, pl.ds(col, w)], wbuf.at[slot, :, pl.ds(k * w, w)], wsem.at[slot, k]
            )
            for k in range(2)
        ]

    def owner(j):
        return place(behind(lax.rem(j, far)), jnp.where(j < far, y, other))

    def downs(q):
        slot = lax.rem(q, SLOTS)
        row = pl.multiple_of(owner(lax.rem(q, n)) * block + (q // n) * w, 128)
        return pltpu.make_async_copy(d_ref.at[pl.ds(row, w), :], dbuf.at[slot], dsem.at[slot])

    def remote(src, dst, send, recv, to):
        return pltpu.make_async_remote_copy(
            src_ref=src, dst_ref=dst, send_sem=send, recv_sem=recv,
            device_id=to, device_id_type=pl.DeviceIdType.MESH,
        )

    def to_near(c, i):
        return remote(ysend.at[c, i], yrecv.at[c, i], ys.at[c, i], yr.at[c, i], near)

    def to_far(c, i):
        return remote(
            yrecv.at[c, i], zrecv.at[c, i], zs.at[c, i], zr.at[c, i], {"gx": place(ahead(i), y)}
        )

    def share_far(c, i):
        return remote(
            hid.at[c, me], hid.at[c, me], gs.at[c, i], gr.at[c, i], {"gx": place(ahead(i), y)}
        )

    def share_near(c, j):
        g = place(behind(j), y)
        return remote(hid.at[c, g], hid.at[c, g], fs.at[c, j], fr.at[c, j], near)

    for t in range(SLOTS):
        for copy in weights(jnp.int32(t)):
            copy.start()
        downs(jnp.int32(t)).start()
    barrier = pltpu.get_barrier_semaphore()
    pl.semaphore_signal(barrier, inc=1, device_id=mate, device_id_type=pl.DeviceIdType.MESH)
    pl.semaphore_signal(barrier, inc=1, device_id=near, device_id_type=pl.DeviceIdType.MESH)
    for i in range(far - 1):
        pl.semaphore_signal(
            barrier, inc=1, device_id={"gx": place(ahead(i), y)}, device_id_type=pl.DeviceIdType.MESH
        )
    tok[core] = tok_in[...].astype(jnp.bfloat16)
    pl.semaphore_wait(barrier, far + 1)
    swap = remote(tok.at[core], tok.at[core], tsem.at[0], tsem.at[1], mate)
    swap.start()
    acc[...] = jnp.zeros_like(acc)
    swap.wait()

    def fetched(t):
        for copy in weights(t):
            copy.wait()

    def fetch_next(t):
        @pl.when(t + SLOTS < 2 * tiles)
        def _():
            for copy in weights(t + SLOTS):
                copy.start()

    def product(t, h):
        return jnp.dot(tok[h], wbuf[lax.rem(t, SLOTS)], preferred_element_type=jnp.float32)

    @pl.loop(0, tiles)
    def _(t):
        c, i = t // far, lax.rem(t, far)
        fetched(t)

        @pl.loop(0, 2)
        def _(h):
            ysend[c, i, h] = product(t, h).astype(jnp.bfloat16)

        to_near(c, i).start()
        fetch_next(t)

    def sums(c):
        @pl.loop(0, far - 1)
        def _(i):
            t = tiles + c * far + i
            fetched(t)
            to_near(c, i).wait_recv()

            @pl.loop(0, 2)
            def _(h):
                both = product(t, h) + yrecv[c, i, h].astype(jnp.float32)
                yrecv[c, i, h] = both.astype(jnp.bfloat16)

            to_far(c, i).start()
            fetch_next(t)

        i = far - 1
        t = jnp.int32(tiles + c * far + i)
        fetched(t)
        to_near(c, i).wait_recv()

        @pl.loop(0, 2)
        def _(h):
            own[c % 2, h] = product(t, h) + yrecv[c, i, h].astype(jnp.float32)

        fetch_next(t)

    def activate(c):
        @pl.loop(0, far - 1)
        def _(i):
            to_far(c, i).wait_recv()

        @pl.loop(0, 2)
        def _(h):
            total = own[c % 2, h]
            for i in range(far - 1):
                total = total + zrecv[c, i, h].astype(jnp.float32)
            gate, up = total[:, :w], total[:, w:]
            hid[c, me, h] = (gate / (1.0 + jnp.exp(-gate)) * up).astype(jnp.bfloat16)

        @pl.loop(0, far - 1)
        def _(i):
            share_far(c, i).start()

        share_near(c, 0).start()

    def forward(c):
        @pl.loop(0, far - 1)
        def _(i):
            share_far(c, i).wait_recv()
            share_near(c, i + 1).start()

    def project(c):
        @pl.loop(0, far)
        def _(j):
            share_near(c, j).wait_recv()

        @pl.loop(0, n)
        def _(j):
            q = c * n + j
            downs(q).wait()

            @pl.loop(0, 2)
            def _(h):
                acc[h] += jnp.dot(
                    hid[c, owner(j), h], dbuf[lax.rem(q, SLOTS)], preferred_element_type=jnp.float32
                )

            @pl.when(q + SLOTS < chunks * n)
            def _():
                downs(q + SLOTS).start()

    for step in range(chunks + 3):
        for lag, stage in enumerate((sums, activate, forward, project)):
            if 0 <= step - lag < chunks:
                stage(step - lag)

    last = remote(acc.at[1 - core], rbuf, osem.at[0], osem.at[1], mate)
    last.start()

    @pl.loop(0, chunks)
    def _(c):
        @pl.loop(0, far)
        def _(i):
            to_near(c, i).wait_send()
            share_near(c, i).wait_send()

        @pl.loop(0, far - 1)
        def _(i):
            to_far(c, i).wait_send()
            share_far(c, i).wait_send()

    last.wait()
    o_ref[...] = acc[core] + rbuf[...]


def shards(n, tokens, gate_up_weight, down_weight):
    rows, depth = tokens.shape
    hidden = gate_up_weight.shape[2]
    width = down_weight.shape[1]
    pair = 2
    far = n // pair
    w = min(WIDTH, hidden // n)
    chunks = hidden // n // w
    bf16, f32 = jnp.bfloat16, jnp.float32
    dma = pltpu.SemaphoreType.DMA
    return pl.pallas_call(
        functools.partial(kernel, n, pair, chunks),
        out_shape=jax.ShapeDtypeStruct((rows, width), f32),
        in_specs=[
            pl.BlockSpec(memory_space=pltpu.VMEM),
            pl.BlockSpec(memory_space=pl.ANY),
            pl.BlockSpec(memory_space=pl.ANY),
        ],
        out_specs=pl.BlockSpec(memory_space=pltpu.VMEM),
        scratch_shapes=[
            pltpu.VMEM((2, rows, depth), bf16),
            pltpu.VMEM((SLOTS, depth, 2 * w), bf16),
            pltpu.VMEM((SLOTS, w, width), bf16),
            pltpu.VMEM((chunks, far, 2, rows, 2 * w), bf16),
            pltpu.VMEM((chunks, far, 2, rows, 2 * w), bf16),
            pltpu.VMEM((chunks, far - 1, 2, rows, 2 * w), bf16),
            pltpu.VMEM((2, 2, rows, 2 * w), f32),
            pltpu.VMEM((chunks, n, 2, rows, w), bf16),
            pltpu.VMEM((2, rows, width), f32),
            pltpu.VMEM((rows, width), f32),
            dma((SLOTS, 2)),
            dma((SLOTS,)),
            dma((2,)),
            dma((chunks, far)),
            dma((chunks, far)),
            dma((chunks, far - 1)),
            dma((chunks, far - 1)),
            dma((chunks, far - 1)),
            dma((chunks, far - 1)),
            dma((chunks, far)),
            dma((chunks, far)),
            dma((2,)),
        ],
        compiler_params=pltpu.CompilerParams(
            collective_id=0, has_side_effects=True, vmem_limit_bytes=60 * 2**20
        ),
    )(tokens, gate_up_weight, down_weight)


def solution(mesh):
    placed = (P(("parts", "gy"), "gx"), P(None, "gx", "gy"), P("gy", "gx"))
    return jax.shard_map(
        functools.partial(shards, mesh.shape["gx"]),
        mesh=mesh, in_specs=placed, out_specs=P(("parts", "gy"), "gx"), check_vma=False,
    )
```

```python
import functools

import jax
import jax.numpy as jnp
from jax import lax
from jax.experimental import pallas as pl
from jax.experimental.pallas import tpu as pltpu
from jax.sharding import PartitionSpec as P

WIDTH = 256
SLOTS = 4
LAGS = (1, 1)


def kernel(
    n, chunks, orders, tok_in, w_ref, d_ref, o_ref,
    tok, wbuf, dbuf, halves, *rest,
):
    bits = n.bit_length() - 1
    levels, rest = rest[:bits], rest[bits:]
    keep, hid, acc, rbuf, wsem, dsem, tsem, osem = rest[:8]
    sends, recvs = rest[8 : 8 + bits], rest[8 + bits : 8 + 2 * bits]
    gs, gr = rest[8 + 2 * bits :]
    w = hid.shape[-1]
    block = chunks * w
    half = n // 2
    tiles = chunks * half
    me = lax.axis_index("gx")
    core = lax.axis_index("gy")
    mate = {"gy": 1 - core}
    mine = [lax.rem(me // 2**k, 2) for k in range(bits)]

    def flip(r):
        return sum(lax.rem(mine[k] + lax.rem(r // 2**k, 2), 2) * 2**k for k in range(bits))

    partner = [{"gx": flip(jnp.int32(2**k))} for k in range(bits)]

    def entry(i):
        return jnp.where(i < half // 2, half - 1 - 2 * i, 2 * half - 2 - 2 * i)

    def weights(t):
        slot = lax.rem(t, SLOTS)
        r = lax.rem(t, tiles)
        e = entry(lax.rem(r, half))
        dest = flip(2 * e + jnp.where(t < tiles, 1, 0))
        col = pl.multiple_of(dest * block + (r // half) * w, 128)
        return [
            pltpu.make_async_copy(
                w_ref.at[k, :, pl.ds(col, w)], wbuf.at[slot, :, pl.ds(k * w, w)], wsem.at[slot, k]
            )
            for k in range(2)
        ]

    def downs(q):
        slot = lax.rem(q, SLOTS)
        copies = []
        for k in range(2):
            r = 2 * lax.rem(q, half) + k
            row = pl.multiple_of(flip(r) * block + (q // half) * w, 128)
            copies.append(
                pltpu.make_async_copy(
                    d_ref.at[pl.ds(row, w), :], dbuf.at[slot, pl.ds(k * w, w), :], dsem.at[slot, k]
                )
            )
        return copies

    def remote(src, dst, send, recv, to):
        return pltpu.make_async_remote_copy(
            src_ref=src, dst_ref=dst, send_sem=send, recv_sem=recv,
            device_id=to, device_id_type=pl.DeviceIdType.MESH,
        )

    def reduce_send(k, c, i):
        src = halves.at[c, i] if k == 0 else levels[k - 1].at[c, 2 * i + 1]
        return remote(src, levels[k].at[c, i], sends[k].at[c, i], recvs[k].at[c, i], partner[k])

    def share(c, r, k):
        to = r ^ 2**k
        return remote(hid.at[c, r], hid.at[c, to], gs.at[c, to], gr.at[c, to], partner[k])

    for t in range(SLOTS):
        for copy in weights(jnp.int32(t)) + downs(jnp.int32(t)):
            copy.start()
    barrier = pltpu.get_barrier_semaphore()
    for to in [mate] + partner:
        pl.semaphore_signal(barrier, inc=1, device_id=to, device_id_type=pl.DeviceIdType.MESH)
    tok[core] = tok_in[...].astype(jnp.bfloat16)
    pl.semaphore_wait(barrier, bits + 1)
    swap = remote(tok.at[core], tok.at[core], tsem.at[0], tsem.at[1], mate)
    swap.start()
    acc[...] = jnp.zeros_like(acc)
    swap.wait()

    def fetched(t):
        for copy in weights(t):
            copy.wait()

    def fetch_next(t):
        @pl.when(t + SLOTS < 2 * tiles)
        def _():
            for copy in weights(t + SLOTS):
                copy.start()

    def product(t, h):
        return jnp.dot(tok[h], wbuf[lax.rem(t, SLOTS)], preferred_element_type=jnp.float32)

    @pl.loop(0, tiles)
    def _(t):
        c, e = t // half, entry(lax.rem(t, half))
        fetched(t)

        @pl.loop(0, 2)
        def _(h):
            halves[c, e, h] = product(t, h).astype(jnp.bfloat16)

        reduce_send(0, c, e).start()
        fetch_next(t)

    def first(c):
        @pl.loop(0, half // 2)
        def _(i):
            t = tiles + c * half + i
            e = entry(i)
            fetched(t)
            reduce_send(0, c, e).wait_recv()

            @pl.loop(0, 2)
            def _(h):
                total = product(t, h) + levels[0][c, e, h].astype(jnp.float32)
                levels[0][c, e, h] = total.astype(jnp.bfloat16)

            reduce_send(1, c, half // 2 - 1 - i).start()
            fetch_next(t)

        @pl.loop(half // 2, half)
        def _(i):
            t = tiles + c * half + i
            e = entry(i)
            fetched(t)
            reduce_send(0, c, e).wait_recv()

            @pl.loop(0, 2)
            def _(h):
                keep[c % 3, half - 1 - i, h] = product(t, h) + levels[0][c, e, h].astype(jnp.float32)

            fetch_next(t)

    def later(k, c):
        count = n >> (k + 1)
        for i in list(range(1, count, 2)) + list(range(0, count, 2)):
            reduce_send(k, c, i).wait_recv()
            at = i << (k - 1)

            @pl.loop(0, 2)
            def _(h):
                total = keep[c % 3, at, h] + levels[k][c, i, h].astype(jnp.float32)
                if k == bits - 1:
                    gate, up = total[:, :w], total[:, w:]
                    hid[c, 0, h] = (gate / (1.0 + jnp.exp(-gate)) * up).astype(jnp.bfloat16)
                elif i % 2:
                    levels[k][c, i, h] = total.astype(jnp.bfloat16)
                else:
                    keep[c % 3, at, h] = total

            if i % 2:
                reduce_send(k + 1, c, i // 2).start()

    def gather(step, c):
        order = orders[c]
        held = [0]
        for k in order[: max(step - 1, 0)]:
            held += [r ^ 2**k for r in held]
        new = [0] if step == 0 else [r ^ 2 ** order[step - 1] for r in held]
        for r in new:
            if step:
                source = order[step - 1]
                share(c, r ^ 2**source, source).wait_recv()
            for k in order[step:]:
                share(c, r, k).start()

    def project(c):
        @pl.loop(0, half)
        def _(j):
            q = c * half + j
            for copy in downs(q):
                copy.wait()

            @pl.loop(0, 2)
            def _(h):
                acc[h] += jnp.dot(
                    jnp.concatenate([hid[c, 2 * j, h], hid[c, 2 * j + 1, h]], axis=1),
                    dbuf[lax.rem(q, SLOTS)],
                    preferred_element_type=jnp.float32,
                )

            @pl.when(q + SLOTS < chunks * half)
            def _():
                for copy in downs(q + SLOTS):
                    copy.start()

    def ended(c):
        gather(bits, c)
        project(c)

    def summed(c):
        for k in range(2, bits):
            later(k, c)
        gather(0, c)

    stages = [first, functools.partial(later, 1), summed]
    stages += [functools.partial(gather, k) for k in range(1, bits)] + [ended]
    lags = [0, LAGS[0], LAGS[1]] + [LAGS[1] + k for k in range(1, bits + 1)]
    for step in range(chunks + lags[-1]):
        for stage, lag in zip(stages, lags):
            if 0 <= step - lag < chunks:
                stage(step - lag)

    last = remote(acc.at[1 - core], rbuf, osem.at[0], osem.at[1], mate)
    last.start()
    for c in range(chunks):
        for k in range(bits):
            for i in range(n >> (k + 1)):
                reduce_send(k, c, i).wait_send()
        for k in orders[c][:1]:
            for to in range(1, n):
                remote(
                    hid.at[c, to], hid.at[c, to], gs.at[c, to], gr.at[c, to], partner[k]
                ).wait_send()
    last.wait()
    o_ref[...] = acc[core] + rbuf[...]


def shards(n, tokens, gate_up_weight, down_weight):
    rows, depth = tokens.shape
    hidden = gate_up_weight.shape[2]
    width = down_weight.shape[1]
    bits = n.bit_length() - 1
    w = min(WIDTH, hidden // n)
    chunks = hidden // n // w
    high = list(range(bits - 1, 0, -1))
    orders = [high + [0]] * chunks
    counts = [n >> (k + 1) for k in range(bits)]
    bf16, f32 = jnp.bfloat16, jnp.float32
    dma = pltpu.SemaphoreType.DMA
    return pl.pallas_call(
        functools.partial(kernel, n, chunks, orders),
        out_shape=jax.ShapeDtypeStruct((rows, width), f32),
        in_specs=[
            pl.BlockSpec(memory_space=pltpu.VMEM),
            pl.BlockSpec(memory_space=pl.ANY),
            pl.BlockSpec(memory_space=pl.ANY),
        ],
        out_specs=pl.BlockSpec(memory_space=pltpu.VMEM),
        scratch_shapes=[
            pltpu.VMEM((2, rows, depth), bf16),
            pltpu.VMEM((SLOTS, depth, 2 * w), bf16),
            pltpu.VMEM((SLOTS, 2 * w, width), bf16),
            pltpu.VMEM((chunks, n // 2, 2, rows, 2 * w), bf16),
            *[pltpu.VMEM((chunks, m, 2, rows, 2 * w), bf16) for m in counts],
            pltpu.VMEM((3, n // 4, 2, rows, 2 * w), f32),
            pltpu.VMEM((chunks, n, 2, rows, w), bf16),
            pltpu.VMEM((2, rows, width), f32),
            pltpu.VMEM((rows, width), f32),
            dma((SLOTS, 2)),
            dma((SLOTS, 2)),
            dma((2,)),
            dma((2,)),
            *[dma((chunks, m)) for m in counts],
            *[dma((chunks, m)) for m in counts],
            dma((chunks, n)),
            dma((chunks, n)),
        ],
        compiler_params=pltpu.CompilerParams(
            collective_id=0, has_side_effects=True, vmem_limit_bytes=60 * 2**20
        ),
    )(tokens, gate_up_weight, down_weight)


def solution(mesh):
    placed = (P(("parts", "gy"), "gx"), P(None, "gx", "gy"), P("gy", "gx"))
    return jax.shard_map(
        functools.partial(shards, mesh.shape["gx"]),
        mesh=mesh, in_specs=placed, out_specs=P(("parts", "gy"), "gx"), check_vma=False,
    )
```

```python
import functools

import jax
import jax.numpy as jnp
from jax import lax
from jax.experimental import pallas as pl
from jax.experimental.pallas import tpu as pltpu
from jax.sharding import PartitionSpec as P

WIDTH = 256
SLOTS = 4
LAGS = (1, 1)


def kernel(
    n, chunks, orders, tok_in, w_ref, d_ref, o_ref,
    tok, wbuf, dbuf, halves, *rest,
):
    bits = n.bit_length() - 1
    levels, rest = rest[:bits], rest[bits:]
    keep, hid, acc, rbuf, wsem, dsem, tsem, osem = rest[:8]
    sends, recvs = rest[8 : 8 + bits], rest[8 + bits : 8 + 2 * bits]
    gs, gr = rest[8 + 2 * bits :]
    w = hid.shape[-1]
    block = chunks * w
    half = n // 2
    tiles = chunks * half
    me = lax.axis_index("gx")
    core = lax.axis_index("gy")
    mate = {"gy": 1 - core}
    mine = [lax.rem(me // 2**k, 2) for k in range(bits)]

    def flip(r):
        return sum(lax.rem(mine[k] + lax.rem(r // 2**k, 2), 2) * 2**k for k in range(bits))

    partner = [{"gx": flip(jnp.int32(2**k))} for k in range(bits)]

    def entry(i):
        return jnp.where(i < half // 2, half - 1 - 2 * i, 2 * half - 2 - 2 * i)

    def weights(t):
        slot = lax.rem(t, SLOTS)
        r = lax.rem(t, tiles)
        e = entry(lax.rem(r, half))
        dest = flip(2 * e + jnp.where(t < tiles, 1, 0))
        col = pl.multiple_of(dest * block + (r // half) * w, 128)
        return [
            pltpu.make_async_copy(
                w_ref.at[k, :, pl.ds(col, w)], wbuf.at[slot, :, pl.ds(k * w, w)], wsem.at[slot, k]
            )
            for k in range(2)
        ]

    def downs(q):
        slot = lax.rem(q, SLOTS)
        copies = []
        for k in range(2):
            r = 2 * lax.rem(q, half) + k
            row = pl.multiple_of(flip(r) * block + (q // half) * w, 128)
            copies.append(
                pltpu.make_async_copy(
                    d_ref.at[pl.ds(row, w), :], dbuf.at[slot, pl.ds(k * w, w), :], dsem.at[slot, k]
                )
            )
        return copies

    def remote(src, dst, send, recv, to):
        return pltpu.make_async_remote_copy(
            src_ref=src, dst_ref=dst, send_sem=send, recv_sem=recv,
            device_id=to, device_id_type=pl.DeviceIdType.MESH,
        )

    def reduce_send(k, c, i):
        src = halves.at[c, i] if k == 0 else levels[k - 1].at[c, 2 * i + 1]
        return remote(src, levels[k].at[c, i], sends[k].at[c, i], recvs[k].at[c, i], partner[k])

    def share(c, r, k):
        to = r ^ 2**k
        return remote(hid.at[c, r], hid.at[c, to], gs.at[c, to], gr.at[c, to], partner[k])

    for t in range(SLOTS):
        for copy in weights(jnp.int32(t)) + downs(jnp.int32(t)):
            copy.start()
    barrier = pltpu.get_barrier_semaphore()
    for to in [mate] + partner:
        pl.semaphore_signal(barrier, inc=1, device_id=to, device_id_type=pl.DeviceIdType.MESH)
    tok[core] = tok_in[...].astype(jnp.bfloat16)
    pl.semaphore_wait(barrier, bits + 1)
    swap = remote(tok.at[core], tok.at[core], tsem.at[0], tsem.at[1], mate)
    swap.start()
    acc[...] = jnp.zeros_like(acc)
    swap.wait()

    def fetched(t):
        for copy in weights(t):
            copy.wait()

    def fetch_next(t):
        @pl.when(t + SLOTS < 2 * tiles)
        def _():
            for copy in weights(t + SLOTS):
                copy.start()

    def product(t, h):
        return jnp.dot(tok[h], wbuf[lax.rem(t, SLOTS)], preferred_element_type=jnp.float32)

    @pl.loop(0, tiles)
    def _(t):
        c, e = t // half, entry(lax.rem(t, half))
        fetched(t)

        @pl.loop(0, 2)
        def _(h):
            halves[c, e, h] = product(t, h).astype(jnp.bfloat16)

        reduce_send(0, c, e).start()
        fetch_next(t)

    def first(c):
        @pl.loop(0, half // 2)
        def _(i):
            t = tiles + c * half + i
            e = entry(i)
            fetched(t)
            reduce_send(0, c, e).wait_recv()

            @pl.loop(0, 2)
            def _(h):
                total = product(t, h) + levels[0][c, e, h].astype(jnp.float32)
                levels[0][c, e, h] = total.astype(jnp.bfloat16)

            reduce_send(1, c, half // 2 - 1 - i).start()
            fetch_next(t)

        @pl.loop(half // 2, half)
        def _(i):
            t = tiles + c * half + i
            e = entry(i)
            fetched(t)
            reduce_send(0, c, e).wait_recv()

            @pl.loop(0, 2)
            def _(h):
                keep[c % 3, half - 1 - i, h] = product(t, h) + levels[0][c, e, h].astype(jnp.float32)

            fetch_next(t)

    def later(k, c):
        count = n >> (k + 1)
        for i in list(range(1, count, 2)) + list(range(0, count, 2)):
            reduce_send(k, c, i).wait_recv()
            at = i << (k - 1)

            @pl.loop(0, 2)
            def _(h):
                total = keep[c % 3, at, h] + levels[k][c, i, h].astype(jnp.float32)
                if k == bits - 1:
                    gate, up = total[:, :w], total[:, w:]
                    hid[c, 0, h] = (gate / (1.0 + jnp.exp(-gate)) * up).astype(jnp.bfloat16)
                elif i % 2:
                    levels[k][c, i, h] = total.astype(jnp.bfloat16)
                else:
                    keep[c % 3, at, h] = total

            if i % 2:
                reduce_send(k + 1, c, i // 2).start()

    def gather(step, c):
        order = orders[c]
        held = [0]
        for k in order[: max(step - 1, 0)]:
            held += [r ^ 2**k for r in held]
        new = [0] if step == 0 else [r ^ 2 ** order[step - 1] for r in held]
        for r in new:
            if step:
                source = order[step - 1]
                share(c, r ^ 2**source, source).wait_recv()
            for k in order[step:]:
                share(c, r, k).start()

    def project(c):
        @pl.loop(0, half)
        def _(j):
            q = c * half + j
            for copy in downs(q):
                copy.wait()

            @pl.loop(0, 2)
            def _(h):
                acc[h] += jnp.dot(
                    jnp.concatenate([hid[c, 2 * j, h], hid[c, 2 * j + 1, h]], axis=1),
                    dbuf[lax.rem(q, SLOTS)],
                    preferred_element_type=jnp.float32,
                )

            @pl.when(q + SLOTS < chunks * half)
            def _():
                for copy in downs(q + SLOTS):
                    copy.start()

    def ended(c):
        gather(bits, c)
        project(c)

    def summed(c):
        for k in range(2, bits):
            later(k, c)
        gather(0, c)

    stages = [first, functools.partial(later, 1), summed]
    stages += [functools.partial(gather, k) for k in range(1, bits)] + [ended]
    lags = [0, LAGS[0], LAGS[1]] + [LAGS[1] + k for k in range(1, bits + 1)]
    for step in range(chunks + lags[-1]):
        for stage, lag in zip(stages, lags):
            if 0 <= step - lag < chunks:
                stage(step - lag)

    last = remote(acc.at[1 - core], rbuf, osem.at[0], osem.at[1], mate)
    last.start()
    for c in range(chunks):
        for k in range(bits):
            for i in range(n >> (k + 1)):
                reduce_send(k, c, i).wait_send()
        for k in orders[c][:1]:
            for to in range(1, n):
                remote(
                    hid.at[c, to], hid.at[c, to], gs.at[c, to], gr.at[c, to], partner[k]
                ).wait_send()
    last.wait()
    o_ref[...] = acc[core] + rbuf[...]


def shards(n, tokens, gate_up_weight, down_weight):
    rows, depth = tokens.shape
    hidden = gate_up_weight.shape[2]
    width = down_weight.shape[1]
    bits = n.bit_length() - 1
    w = min(WIDTH, hidden // n)
    chunks = hidden // n // w
    high = list(range(bits - 1, 0, -1))
    orders = [high + [0]] * (chunks - 1) + [[0] + high]
    counts = [n >> (k + 1) for k in range(bits)]
    bf16, f32 = jnp.bfloat16, jnp.float32
    dma = pltpu.SemaphoreType.DMA
    return pl.pallas_call(
        functools.partial(kernel, n, chunks, orders),
        out_shape=jax.ShapeDtypeStruct((rows, width), f32),
        in_specs=[
            pl.BlockSpec(memory_space=pltpu.VMEM),
            pl.BlockSpec(memory_space=pl.ANY),
            pl.BlockSpec(memory_space=pl.ANY),
        ],
        out_specs=pl.BlockSpec(memory_space=pltpu.VMEM),
        scratch_shapes=[
            pltpu.VMEM((2, rows, depth), bf16),
            pltpu.VMEM((SLOTS, depth, 2 * w), bf16),
            pltpu.VMEM((SLOTS, 2 * w, width), bf16),
            pltpu.VMEM((chunks, n // 2, 2, rows, 2 * w), bf16),
            *[pltpu.VMEM((chunks, m, 2, rows, 2 * w), bf16) for m in counts],
            pltpu.VMEM((3, n // 4, 2, rows, 2 * w), f32),
            pltpu.VMEM((chunks, n, 2, rows, w), bf16),
            pltpu.VMEM((2, rows, width), f32),
            pltpu.VMEM((rows, width), f32),
            dma((SLOTS, 2)),
            dma((SLOTS, 2)),
            dma((2,)),
            dma((2,)),
            *[dma((chunks, m)) for m in counts],
            *[dma((chunks, m)) for m in counts],
            dma((chunks, n)),
            dma((chunks, n)),
        ],
        compiler_params=pltpu.CompilerParams(
            collective_id=0, has_side_effects=True, vmem_limit_bytes=60 * 2**20
        ),
    )(tokens, gate_up_weight, down_weight)


def solution(mesh):
    placed = (P(("parts", "gy"), "gx"), P(None, "gx", "gy"), P("gy", "gx"))
    return jax.shard_map(
        functools.partial(shards, mesh.shape["gx"]),
        mesh=mesh, in_specs=placed, out_specs=P(("parts", "gy"), "gx"), check_vma=False,
    )
```
